32 devices in a mesh: ka: 8 (over z, y), ga: 4 (over x, core).
Axes of the slice: x: 2, y: 2, z: 4, core: 2. Of those that a mesh axis runs over, the one named last changes fastest.
Arguments:
- cond_pairs: bfloat16 [4, 48, 2, 16, 1024], P(None, 'ka', None, None, 'ga'), may hold values from -1 to 1
- val_pairs: bfloat16 [4, 48, 2, 16, 1024], P(None, 'ka', None, None, 'ga'), may hold values from -1 to 1
- screened: bfloat16 [4, 2, 1024, 1024], P(None, None, 'ka', 'ga'), may hold values from -1 to 4, as said below
- k_plus: int32 [4, 48], replicated, may hold values from 0 to 47, as said below
Outputs:
- kernel_forward: float32 [4, 48, 2, 256], P(None, 'ka', None, 'ga')
- kernel_back: float32 [4, 48, 2, 256], P(None, 'ka', None, 'ga')
The draws below stay inside these ranges and needn't reach their ends.
Inputs may be any that keep to these rules, and one draw needn't show every extreme that they name: screened[q, 0] is symmetric and screened[q, 1] antisymmetric in the last two dimensions, so W(q) is Hermitian. For each q there is one translation (dx, dy) of the periodic 4 x 12 grid, with k = x * 12 + y, such that k_plus[q, k] = ((x + dx) mod 4) * 12 + (y + dy) mod 12.
All inputs are finite; a program needn't handle non-finite values.
Results may differ from the reference program's by a relative error of at most 0.0029.
Values may be sent and summed in bfloat16 or wider, within the bound.
A program may use at most 64 MiB of HBM per device.

```python
import jax
import jax.numpy as jnp
from jax import lax

NG = 1024
Q = 4
K_DEV = 6
CPAIR = 16
VPAIR = 16
KY = 12
KX = 4
NK = 48
N_KA = 8


def draw_screened(key, part):
    base = jax.random.fold_in(key, 7)
    diag_key, real_key, imag_key = jax.random.split(base, 3)
    diagonal = jnp.exp(jax.random.uniform(diag_key, (Q, NG), jnp.float32, -0.7, 0.7))
    raw_real = jax.random.truncated_normal(real_key, -4.0, 4.0, (Q, NG, NG), jnp.float32)
    raw_imag = jax.random.truncated_normal(imag_key, -4.0, 4.0, (Q, NG, NG), jnp.float32)
    factor = 0.35 / jnp.sqrt(jnp.float32(NG))
    identity_grid = jnp.eye(NG, dtype=jnp.float32)
    real_part = (raw_real + jnp.swapaxes(raw_real, 1, 2)) * factor + diagonal[:, :, None] * identity_grid[None]
    imag_part = (raw_imag - jnp.swapaxes(raw_imag, 1, 2)) * factor
    return jnp.stack([real_part, imag_part], 1).astype(jnp.bfloat16)


def draw_k_plus(key, part):
    base = jax.random.fold_in(key, 13)
    row_key, col_key = jax.random.split(base)
    row_step = jax.random.randint(row_key, (Q,), 1, KX)
    col_step = jax.random.randint(col_key, (Q,), 1, KY)
    points = jnp.arange(NK, dtype=jnp.int32)
    grid_row = points // KY
    grid_col = points % KY
    new_row = (grid_row[None, :] + row_step[:, None]) % KX
    new_col = (grid_col[None, :] + col_step[:, None]) % KY
    return (new_row * KY + new_col).astype(jnp.int32)


def levels(stream_key, shape, shards, least, high):
    def one(position, parts):
        draws = jax.random.uniform(jax.random.fold_in(jax.random.fold_in(stream_key, 6), position), (parts,), jnp.float32, least / len(shards), high / len(shards))
        return jnp.repeat(jnp.exp(draws), shape[position] // parts).reshape((-1,) + (1,) * (len(shape) - position - 1))

    loudness = one(*shards[0])
    for cut in shards[1:]:
        loudness = loudness * one(*cut)
    return loudness


def normal_values(rng, extent, scale, most, pieces=(), kind=jnp.bfloat16):
    drawn = scale * jax.random.normal(rng, extent, jnp.float32)
    if pieces:
        drawn = drawn * levels(rng, extent, pieces, -0.22, 0.18)
    return jnp.clip(drawn, -most, most).astype(kind)


def setup_inputs(seed: int = 0) -> dict:
    arg_keys = jax.random.split(jax.random.key(seed), 5)
    cond_pairs = normal_values(arg_keys[0], (Q, NK, 2, CPAIR, NG), (1.0 / NG ** 0.25), 1.0, ((1, 8), (4, 4)))
    val_pairs = normal_values(arg_keys[1], (Q, NK, 2, VPAIR, NG), (1.0 / NG ** 0.25), 1.0, ((1, 8), (4, 4)))
    screened = draw_screened(jax.random.fold_in(arg_keys[4], 71), 0)
    k_plus = draw_k_plus(jax.random.fold_in(arg_keys[4], 71), 0)
    return dict(cond_pairs=cond_pairs, val_pairs=val_pairs, screened=screened, k_plus=k_plus)


def pair_einsum(left, right):
    return jnp.einsum("kag,kbg->kab", left, right)


def block_kernel(cond, val, w_real, w_imag):
    count = cond.shape[0]
    left_real = cond[:, 0].reshape(count * CPAIR, NG)
    left_imag = cond[:, 1].reshape(count * CPAIR, NG)
    real_x = jnp.dot(left_real, w_real, preferred_element_type=jnp.float32) + jnp.dot(left_imag, w_imag, preferred_element_type=jnp.float32)
    imag_x = jnp.dot(left_real, w_imag, preferred_element_type=jnp.float32) - jnp.dot(left_imag, w_real, preferred_element_type=jnp.float32)
    real_b = lax.optimization_barrier(real_x.astype(jnp.bfloat16)).astype(jnp.float32).reshape(count, CPAIR, NG)
    imag_b = lax.optimization_barrier(imag_x.astype(jnp.bfloat16)).astype(jnp.float32).reshape(count, CPAIR, NG)
    val_real = val[:, 0].astype(jnp.float32)
    val_imag = val[:, 1].astype(jnp.float32)
    kernel_real = pair_einsum(real_b, val_real) - pair_einsum(imag_b, val_imag)
    kernel_imag = pair_einsum(real_b, val_imag) + pair_einsum(imag_b, val_real)
    return jnp.stack([kernel_real, kernel_imag], 1).reshape(count, 2, CPAIR * VPAIR)


def reference(cond_pairs, val_pairs, screened, k_plus):
    forwards = []
    backs = []
    for q_index in range(Q):
        cond = cond_pairs[q_index].reshape(N_KA, K_DEV, 2, CPAIR, NG)
        val = val_pairs[q_index].reshape(N_KA, K_DEV, 2, VPAIR, NG)
        w_real = screened[q_index, 0]
        w_imag = screened[q_index, 1]
        blocks = lax.map(lambda both: block_kernel(both[0], both[1], w_real, w_imag), (cond, val))
        forward = blocks.reshape(NK, 2, CPAIR * VPAIR)
        source = jnp.zeros((NK,), jnp.int32).at[k_plus[q_index].astype(jnp.int32)].set(jnp.arange(NK, dtype=jnp.int32))
        forwards.append(forward)
        backs.append(forward[source])
    return jnp.stack(forwards, 0), jnp.stack(backs, 0)
```

```python
import functools

import jax
import jax.numpy as jnp
from jax import lax
from jax.experimental import pallas as pl
from jax.experimental.pallas import tpu as pltpu
from jax.sharding import PartitionSpec as P

MESH = pl.DeviceIdType.MESH
HIGHEST = lax.Precision.HIGHEST
F32 = jnp.float32
BF16 = jnp.bfloat16


def nearest_source(pair, dest):
    i, j = pair
    if abs(i - dest) == abs(j - dest):
        return i if i in (0,) or j == dest + 1 and i == dest - 1 and dest < 2 else j
    return i if abs(i - dest) < abs(j - dest) else j


def block_plan(rows):
    squares, others = [], []
    for dest in range(rows):
        squares.append(sorted(((i, i) for i in range(rows) if i != dest), key=lambda b: abs(b[0] - dest)))
        blocks = []
        for i in range(rows):
            for j in range(i + 1, rows):
                if dest not in (i, j):
                    src = nearest_source((i, j), dest)
                    blocks.append((src, i + j - src))
        others.append(sorted(blocks, key=lambda b: abs(b[0] - dest)))
    return squares, others


def pick(index, values):
    out = jnp.int32(values[0])
    for n in range(1, len(values)):
        out = jnp.where(index == n, jnp.int32(values[n]), out)
    return out


def nt(a, b):
    return lax.dot_general(a, b, (((1,), (1,)), ((), ())), preferred_element_type=F32)


def kernel(
    rows, c_ref, v_ref, w_ref, kp_ref, f_ref, b_ref,
    wall, cbuf, vbuf, lhs, mix, vl, xacc, kown, ksib, kstage, kall,
    w1s, w1r, cs, cr, vs, vr, cfs, vfs, zs, zr, ks, kr, os, orr,
):
    kpd, npair = cbuf.shape[2], cbuf.shape[4]
    half = wall.shape[3]
    mrows = 2 * kpd * npair
    ka, g = lax.axis_index("ka"), lax.axis_index("ga")
    z, y = ka // 2, ka % 2
    x, h = g // 2, g % 2
    mine = 2 * x + y

    def dev(zz, yy, xx, hh):
        return (2 * zz + yy, 2 * xx + hh)

    def remote(src, dst, ssem, rsem, target):
        return pltpu.make_async_remote_copy(
            src_ref=src, dst_ref=dst, send_sem=ssem, recv_sem=rsem, device_id=target, device_id_type=MESH
        )

    barrier = pltpu.get_barrier_semaphore()
    count = 0
    for dz in range(rows):
        for dy in range(2):
            for dx in range(2):
                for dh in range(2):
                    if (dz and dh) or not (dz or dy or dx or dh):
                        continue
                    pl.semaphore_signal(
                        barrier, inc=1,
                        device_id=dev((z + dz) % rows, (y + dy) % 2, (x + dx) % 2, (h + dh) % 2),
                        device_id_type=MESH,
                    )
                    count += 1
    pl.semaphore_wait(barrier, count)

    steps = [(1, 1), (1, 0), (0, 1), (0, 0)]

    def w_copy(n):
        dy, dx = steps[n]
        qy, qx = (y + dy) % 2, (x + dx) % 2
        return remote(w_ref.at[2 * qx + qy], wall.at[z, g], w1s.at[n], w1r.at[g], dev(z, qy, qx, y))

    for n in range(3):
        w_copy(n).start()

    @pl.when(h == y)
    def _():
        pltpu.make_async_copy(w_ref.at[mine], wall.at[z, g], w1r.at[g]).start()

    @pl.when(h != y)
    def _():
        w_copy(3).start()

    def pair_copy(ref, buf, ssem, rsem, n):
        dy, dx = steps[n]
        qy, qx = (y + dy) % 2, (x + dx) % 2
        return remote(ref.at[2 * qx + qy], buf.at[y, g], ssem.at[n], rsem.at[y, g], dev(z, qy, qx, h))

    xacc[...] = jnp.zeros_like(xacc)

    for j in range(rows):
        pltpu.make_async_copy(wall.at[z, j], wall.at[z, j], w1r.at[j]).wait()

    squares, others = block_plan(rows)
    sends = [[] for _ in range(rows)]
    for dest in range(rows):
        for i, j in squares[dest] + others[dest]:
            sends[i].append((dest, j))

    def z_copies(src):
        order = sorted(sends[src], key=lambda s: (abs(s[0] - src), s[1] == src))
        for n, (dest, j) in enumerate(order):
            yield remote(wall.at[src, j], wall.at[src, j], zs.at[n], zr.at[src, j], dev(dest, y, x, h))

    for src in range(rows):
        @pl.when(z == src)
        def _():
            for copy in z_copies(src):
                copy.start()

    for ref, buf, ssem, rsem in ((c_ref, cbuf, cs, cr), (v_ref, vbuf, vs, vr)):
        for n in range(3):
            pair_copy(ref, buf, ssem, rsem, n).start()
        pltpu.make_async_copy(ref.at[mine], buf.at[y, g], rsem.at[y, g]).start()

    def hand_on(buf, ssem, rsem, yy, xx):
        slot = buf.at[yy, 2 * xx + h]
        return remote(slot, slot, ssem.at[yy, xx], rsem.at[yy, 2 * xx + h], dev(z, y, x, 1 - h))

    def arrived(buf, rsem, yy, j):
        pltpu.make_async_copy(buf.at[yy, j], buf.at[yy, j], rsem.at[yy, j]).wait()

    for buf, rsem, fsem in ((cbuf, cr, cfs), (vbuf, vr, vfs)):
        for dy in range(2):
            for dx in range(2):
                yy, xx = (y + dy) % 2, (x + dx) % 2
                arrived(buf, rsem, yy, 2 * xx + h)
                hand_on(buf, fsem, rsem, yy, xx).start()

    def stacked(buf, rsem, out):
        for yy in range(2):
            for xx in range(2):
                arrived(buf, rsem, yy, 2 * xx + 1 - h)
        for j in range(rows):
            for yy in range(2):
                for part in range(2):
                    block = buf[yy, j, :, part].reshape(kpd * npair, 2 * half)
                    out[j, pl.ds((2 * part + yy) * kpd * npair, kpd * npair), :] = block

    lanes = pl.ds(pl.multiple_of(h * half, half), half)
    stacked(cbuf, cr, lhs)
    for j in range(rows):
        both = lhs[j, :, lanes]
        real, imag = both[:mrows], both[mrows:]
        mix[j, :mrows, :half] = real
        mix[j, :mrows, half:] = imag
        mix[j, mrows:, :half] = -imag
        mix[j, mrows:, half:] = real

    def plain(i, j):
        w = wall[i, j].reshape(2 * half, 2 * half)
        xacc[j] += jnp.dot(mix[i], w, preferred_element_type=F32)

    def adjoint(i, j):
        w = wall[i, j].reshape(2 * half, 2 * half)
        p = nt(lhs[j], w)
        xacc[i, :mrows, lanes] += p[:mrows, :half] - p[mrows:, half:]
        xacc[i, mrows:, lanes] -= p[:mrows, half:] + p[mrows:, :half]

    plain(z, z)
    for n in range(1, rows):
        j = (z + n) % rows
        plain(z, j)
        adjoint(z, j)

    stacked(vbuf, vr, vl)

    nsq, noth = len(squares[0]), len(others[0])
    for n in range(max(nsq, noth)):
        if n < nsq:
            i = pick(z, [s[n][0] for s in squares])
            pltpu.make_async_copy(wall.at[i, i], wall.at[i, i], zr.at[i, i]).wait()
            plain(i, i)
        if n < noth:
            i = pick(z, [s[n][0] for s in others])
            j = pick(z, [s[n][1] for s in others])
            pltpu.make_async_copy(wall.at[i, j], wall.at[i, j], zr.at[i, j]).wait()
            plain(i, j)
            adjoint(i, j)

    with_real = jnp.zeros((2 * mrows, mrows), F32)
    with_imag = jnp.zeros((2 * mrows, mrows), F32)
    for j in range(rows):
        total = xacc[j]
        high = total.astype(BF16)
        low = (total - high.astype(F32)).astype(BF16)
        vreal, vimag = vl[j, :mrows], vl[j, mrows:]
        with_real += nt(high, vreal) + nt(low, vreal)
        with_imag += nt(high, vimag) + nt(low, vimag)
    kreal = with_real[:mrows] - with_imag[mrows:]
    kimag = with_imag[:mrows] + with_real[mrows:]

    width = npair * npair
    row = lax.broadcasted_iota(jnp.int32, (mrows, mrows), 0)
    col = lax.broadcasted_iota(jnp.int32, (mrows, mrows), 1)
    same_k = lax.div(row, npair) == lax.div(col, npair)
    vrow = lax.broadcasted_iota(jnp.int32, (mrows, width), 0)
    lane = lax.broadcasted_iota(jnp.int32, (mrows, width), 1)
    spread = jnp.where(lax.rem(vrow, npair) == lax.rem(lane, npair), 1.0, 0.0).astype(F32)
    same_a = lax.rem(vrow, npair) == lax.div(lane, npair)
    kgrid = mrows // npair
    for part, value in enumerate((kreal, kimag)):
        wide = jnp.dot(jnp.where(same_k, value, 0.0), spread, precision=HIGHEST, preferred_element_type=F32)
        wide = jnp.where(same_a, wide, 0.0).reshape(kgrid, npair, width)
        kown[pl.ds(part * kgrid, kgrid), :] = wide.sum(1)

    pair_sum = remote(kown, ksib, ks, kr, dev(z, y, x, 1 - h))
    pair_sum.start()
    pair_sum.wait()
    total = kown[...] + ksib[...]
    share = kstage.shape[2]
    for n in range(kstage.shape[0]):
        kstage[n] = total[:, n * share:(n + 1) * share]

    def out_copies():
        n = 0
        for dz in range(rows):
            for dy in range(2):
                for dx in range(2):
                    if dz or dy or dx:
                        zz, yy, xx = (z + dz) % rows, (y + dy) % 2, (x + dx) % 2
                        yield remote(
                            kstage.at[2 * xx + h], kall.at[mine, z], os.at[n], orr.at[mine, z], dev(zz, yy, xx, h)
                        )
                        n += 1

    for copy in out_copies():
        copy.start()
    kall[mine, z] = kstage[g]
    for dz in range(rows):
        for dy in range(2):
            for dx in range(2):
                if dz or dy or dx:
                    zz = (z + dz) % rows
                    qq = 2 * ((x + dx) % 2) + (y + dy) % 2
                    pltpu.make_async_copy(kall.at[qq, zz], kall.at[qq, zz], orr.at[qq, zz]).wait()

    outs = f_ref.shape[1]
    o = lax.broadcasted_iota(jnp.int32, (outs, rows * 2 * kgrid), 0)
    r = lax.broadcasted_iota(jnp.int32, (outs, rows * 2 * kgrid), 1)
    k_here = y * kpd + lax.div(o, 2)
    part_at = lax.rem(o, 2) * kgrid
    ahead = jnp.where(r == z * 2 * kgrid + part_at + k_here, 1.0, 0.0).astype(F32)
    for q in range(kall.shape[0]):
        table = kall[q].reshape(rows * 2 * kgrid, share)
        corner = kp_ref[q, 0]
        row_step = lax.div(corner, kgrid)
        col_step = lax.rem(corner, kgrid)
        src_row = lax.rem(z - row_step + rows, rows)
        src_col = lax.rem(k_here - col_step + kgrid, kgrid)
        behind = jnp.where(r == src_row * 2 * kgrid + part_at + src_col, 1.0, 0.0).astype(F32)
        f_ref[q] = jnp.dot(ahead, table, precision=HIGHEST, preferred_element_type=F32)
        b_ref[q] = jnp.dot(behind, table, precision=HIGHEST, preferred_element_type=F32)

    for n in range(3):
        w_copy(n).wait_send()
        pair_copy(c_ref, cbuf, cs, cr, n).wait_send()
        pair_copy(v_ref, vbuf, vs, vr, n).wait_send()

    @pl.when(h != y)
    def _():
        w_copy(3).wait_send()

    for src in range(rows):
        @pl.when(z == src)
        def _():
            for copy in z_copies(src):
                copy.wait_send()

    for buf, rsem, fsem in ((cbuf, cr, cfs), (vbuf, vr, vfs)):
        for dy in range(2):
            for dx in range(2):
                hand_on(buf, fsem, rsem, (y + dy) % 2, (x + dx) % 2).wait_send()
    for copy in out_copies():
        copy.wait_send()


def exchanged(cond_pairs, val_pairs, screened, k_plus):
    nq, kpd, _, npair, cols = cond_pairs.shape
    half = screened.shape[2]
    rows = lax.axis_size("ka") // 2
    ga = lax.axis_size("ga")
    mrows = 2 * kpd * npair
    width = npair * npair
    share = width // ga
    dma = pltpu.SemaphoreType.DMA
    out = jax.ShapeDtypeStruct((nq, 2 * kpd, share), F32)
    squares, others = block_plan(rows)
    most = max(
        sum(i == src for d in range(rows) for i, _ in squares[d] + others[d]) for src in range(rows)
    )
    forward, back = pl.pallas_call(
        functools.partial(kernel, rows),
        out_shape=(out, out),
        in_specs=[pl.BlockSpec(memory_space=pl.ANY)] * 3 + [pl.BlockSpec(memory_space=pltpu.SMEM)],
        out_specs=[pl.BlockSpec(memory_space=pltpu.VMEM)] * 2,
        scratch_shapes=[
            pltpu.VMEM((rows, rows, 2, half, cols), BF16),
            pltpu.VMEM((2, ga, kpd, 2, npair, cols), BF16),
            pltpu.VMEM((2, ga, kpd, 2, npair, cols), BF16),
            pltpu.VMEM((ga, 2 * mrows, cols), BF16),
            pltpu.VMEM((ga, 2 * mrows, cols), BF16),
            pltpu.VMEM((ga, 2 * mrows, cols), BF16),
            pltpu.VMEM((ga, 2 * mrows, cols), F32),
            pltpu.VMEM((4 * kpd, width), F32),
            pltpu.VMEM((4 * kpd, width), F32),
            pltpu.VMEM((ga, 4 * kpd, share), F32),
            pltpu.VMEM((nq, rows, 4 * kpd, share), F32),
            dma((4,)), dma((ga,)),
            dma((3,)), dma((2, ga)),
            dma((3,)), dma((2, ga)),
            dma((2, 2)), dma((2, 2)),
            dma((most,)), dma((rows, rows)),
            dma, dma,
            dma((4 * rows - 1,)), dma((nq, rows)),
        ],
        compiler_params=pltpu.CompilerParams(
            collective_id=0, has_side_effects=True, vmem_limit_bytes=40 * 1024 * 1024
        ),
    )(cond_pairs, val_pairs, screened, k_plus)
    shape = (nq, kpd, 2, share)
    return forward.reshape(shape), back.reshape(shape)


NG = 1024
Q = 4
npair = 16
npair = 16


def passed_along(block, axis, distance):
    devices = range(lax.axis_size(axis))
    route = [((i - distance) % len(devices), i) for i in devices]
    return lax.ppermute(block, axis, route)


def swapped(shard, axis, bit):
    return lax.ppermute(shard, axis, [(i, i ^ 1 << bit) for i in range(lax.axis_size(axis))])


def screen_fold(left_real, left_imag, piece):
    real_next = jnp.dot(left_real, piece[0], preferred_element_type=jnp.float32) + jnp.dot(
        left_imag, piece[1], preferred_element_type=jnp.float32
    )
    imag_next = jnp.dot(left_real, piece[1], preferred_element_type=jnp.float32) - jnp.dot(
        left_imag, piece[0], preferred_element_type=jnp.float32
    )
    return (real_next, imag_next)


def pair_contract(left, right):
    return jnp.einsum("kag,kbg->kab", left, right, preferred_element_type=jnp.float32)


def local(cond_pairs, val_pairs, screened, k_plus):
    nq, local_k, _, npair, own = cond_pairs.shape
    ng = own * lax.axis_size("ga")
    columns = screened.shape[3]
    grid_y = 2 * local_k
    forward = []
    for q_index in range(nq):
        cond_full = lax.all_gather(cond_pairs[q_index], "ga", axis=3, tiled=True)
        left_real = cond_full[:, 0].reshape(local_k * npair, ng)
        left_imag = cond_full[:, 1].reshape(local_k * npair, ng)
        real_x, imag_x = screen_fold(
            left_real, left_imag, lax.all_gather(screened[q_index], "ka", axis=1, tiled=True)
        )
        real_b = real_x.astype(jnp.bfloat16).reshape(local_k, npair, columns)
        imag_b = imag_x.astype(jnp.bfloat16).reshape(local_k, npair, columns)
        val_real = val_pairs[q_index][:, 0]
        val_imag = val_pairs[q_index][:, 1]
        kernel_real = pair_contract(real_b, val_real) - pair_contract(imag_b, val_imag)
        kernel_imag = pair_contract(real_b, val_imag) + pair_contract(imag_b, val_real)
        forward.append(jnp.stack([kernel_real, kernel_imag], 1).reshape(local_k, 2, npair * npair))
    partial_value = jnp.stack(forward, 0)
    total = lax.psum(partial_value, "ga")
    width = total.shape[3] // lax.axis_size("ga")
    kernel_share = lax.dynamic_slice_in_dim(total, lax.axis_index("ga") * width, width, 3)
    count = lax.axis_size("ka")
    corner = k_plus[:, 0]
    row_step = corner // grid_y
    col_step = corner % grid_y
    hop_length = 2 * row_step % count
    moved = kernel_share
    nbits = count.bit_length() - 1
    for bit_number in range(1, nbits):
        arrived = passed_along(moved, "ka", 1 << bit_number)
        taken = hop_length // (1 << bit_number) % 2 == 1
        moved = jnp.where(taken[:, None, None, None], arrived, moved)
    partner = swapped(moved, "ka", 0)
    half_index = lax.axis_index("ka") % 2
    whole_row = jnp.where(
        half_index == 0, jnp.concatenate([moved, partner], 1), jnp.concatenate([partner, moved], 1)
    )
    doubled = jnp.concatenate([whole_row, whole_row], 1)
    backs = []
    for q_index in range(nq):
        begin = (half_index * local_k - col_step[q_index] + grid_y) % grid_y
        backs.append(lax.dynamic_slice_in_dim(doubled[q_index], begin, local_k, 0))
    kernel_back = jnp.stack(backs, 0)
    return (kernel_share, kernel_back)


def solution(mesh):
    in_specs = (
        P(None, "ka", None, None, "ga"),
        P(None, "ka", None, None, "ga"),
        P(None, None, "ka", "ga"),
        P(),
    )
    out_specs = (P(None, "ka", None, "ga"), P(None, "ka", None, "ga"))
    square = mesh.shape["ga"] == 4 and mesh.shape["ka"] == 2 * mesh.shape["ga"]
    body = exchanged if square else local
    return jax.shard_map(body, mesh=mesh, in_specs=in_specs, out_specs=out_specs, check_vma=False)
```

```python
import functools

import jax
import jax.numpy as jnp
from jax import lax
from jax.experimental import pallas as pl
from jax.experimental.pallas import tpu as pltpu
from jax.sharding import PartitionSpec as P

MESH = pl.DeviceIdType.MESH
HIGHEST = lax.Precision.HIGHEST
F32 = jnp.float32
BF16 = jnp.bfloat16


def nearest_source(pair, dest):
    i, j = pair
    if abs(i - dest) == abs(j - dest):
        return i if i == 0 else j
    return i if abs(i - dest) < abs(j - dest) else j


def block_plan(rows):
    squares, others = [], []
    for dest in range(rows):
        squares.append(sorted(((i, i) for i in range(rows) if i != dest), key=lambda b: abs(b[0] - dest)))
        blocks = []
        for i in range(rows):
            for j in range(i + 1, rows):
                if dest not in (i, j):
                    src = nearest_source((i, j), dest)
                    blocks.append((src, i + j - src))
        others.append(sorted(blocks, key=lambda b: abs(b[0] - dest)))
    return squares, others


def pick(index, values):
    out = jnp.int32(values[0])
    for n in range(1, len(values)):
        out = jnp.where(index == n, jnp.int32(values[n]), out)
    return out


def nt(a, b):
    return lax.dot_general(a, b, (((1,), (1,)), ((), ())), preferred_element_type=F32)


def kernel(
    rows, c_ref, v_ref, w_ref, kp_ref, f_ref, b_ref,
    wall, packed, cbuf, vbuf, lhs, mix, vl, xacc, kown, ksib, kstage, kall,
    w1s, w1r, cs, cr, vs, vr, cfs, vfs, zs, zr, ks, kr, os, orr,
):
    kpd, npair = cbuf.shape[2], cbuf.shape[4]
    half = wall.shape[3]
    mrows = 2 * kpd * npair
    ka, g = lax.axis_index("ka"), lax.axis_index("ga")
    z, y = ka // 2, ka % 2
    x, h = g // 2, g % 2
    mine = 2 * x + y

    def dev(zz, yy, xx, hh):
        return (2 * zz + yy, 2 * xx + hh)

    def remote(src, dst, ssem, rsem, target):
        return pltpu.make_async_remote_copy(
            src_ref=src, dst_ref=dst, send_sem=ssem, recv_sem=rsem, device_id=target, device_id_type=MESH
        )

    barrier = pltpu.get_barrier_semaphore()
    count = 0
    for dz in range(rows):
        for dy in range(2):
            for dx in range(2):
                for dh in range(2):
                    if (dz and dh) or not (dz or dy or dx or dh):
                        continue
                    pl.semaphore_signal(
                        barrier, inc=1,
                        device_id=dev((z + dz) % rows, (y + dy) % 2, (x + dx) % 2, (h + dh) % 2),
                        device_id_type=MESH,
                    )
                    count += 1
    pl.semaphore_wait(barrier, count)

    steps = [(1, 1), (1, 0), (0, 1), (0, 0)]

    def w_copy(n):
        dy, dx = steps[n]
        qy, qx = (y + dy) % 2, (x + dx) % 2
        return remote(w_ref.at[2 * qx + qy], wall.at[z, g], w1s.at[n], w1r.at[g], dev(z, qy, qx, y))

    for n in range(3):
        w_copy(n).start()

    @pl.when(h == y)
    def _():
        pltpu.make_async_copy(w_ref.at[mine], wall.at[z, g], w1r.at[g]).start()

    @pl.when(h != y)
    def _():
        w_copy(3).start()

    def pair_copy(ref, buf, ssem, rsem, n):
        dy, dx = steps[n]
        qy, qx = (y + dy) % 2, (x + dx) % 2
        return remote(ref.at[2 * qx + qy], buf.at[y, g], ssem.at[n], rsem.at[y, g], dev(z, qy, qx, h))

    xacc[...] = jnp.zeros_like(xacc)

    squares, others = block_plan(rows)
    sends = [[] for _ in range(rows)]
    for dest in range(rows):
        for i, j in squares[dest] + others[dest]:
            sends[i].append((dest, j))

    at_row = h * half + lax.broadcasted_iota(jnp.int32, (half, 2 * half), 0)
    at_col = lax.broadcasted_iota(jnp.int32, (half, 2 * half), 1)

    def z_copies(src, which=None):
        order = sorted(sends[src], key=lambda s: (s[1], -abs(s[0] - src)))
        for n, (dest, j) in enumerate(order):
            if which is None or j == which:
                ref = packed.at[src] if j == src else wall.at[src, j]
                yield remote(ref, ref, zs.at[n], zr.at[src, j], dev(dest, y, x, h))

    for j in range(rows):
        pltpu.make_async_copy(wall.at[z, j], wall.at[z, j], w1r.at[j]).wait()
        for src in range(rows):
            @pl.when(z == src)
            def _():
                if j == src:
                    upper = at_col >= at_row
                    packed[src] = jnp.where(
                        upper, wall[src, src, 0].astype(F32), wall[src, src, 1].astype(F32)
                    ).astype(BF16)
                for copy in z_copies(src, j):
                    copy.start()

    for ref, buf, ssem, rsem in ((c_ref, cbuf, cs, cr), (v_ref, vbuf, vs, vr)):
        for n in range(3):
            pair_copy(ref, buf, ssem, rsem, n).start()
        pltpu.make_async_copy(ref.at[mine], buf.at[y, g], rsem.at[y, g]).start()

    def hand_on(buf, ssem, rsem, yy, xx):
        slot = buf.at[yy, 2 * xx + h]
        return remote(slot, slot, ssem.at[yy, xx], rsem.at[yy, 2 * xx + h], dev(z, y, x, 1 - h))

    def arrived(buf, rsem, yy, j):
        pltpu.make_async_copy(buf.at[yy, j], buf.at[yy, j], rsem.at[yy, j]).wait()

    for buf, rsem, fsem in ((cbuf, cr, cfs), (vbuf, vr, vfs)):
        for dy in range(2):
            for dx in range(2):
                yy, xx = (y + dy) % 2, (x + dx) % 2
                arrived(buf, rsem, yy, 2 * xx + h)
                hand_on(buf, fsem, rsem, yy, xx).start()

    def stacked(buf, rsem, out):
        for yy in range(2):
            for xx in range(2):
                arrived(buf, rsem, yy, 2 * xx + 1 - h)
        for j in range(rows):
            for yy in range(2):
                for part in range(2):
                    block = buf[yy, j, :, part].reshape(kpd * npair, 2 * half)
                    out[j, pl.ds((2 * part + yy) * kpd * npair, kpd * npair), :] = block

    lanes = pl.ds(pl.multiple_of(h * half, half), half)
    stacked(cbuf, cr, lhs)
    for j in range(rows):
        both = lhs[j, :, lanes]
        real, imag = both[:mrows], both[mrows:]
        mix[j, :mrows, :half] = real
        mix[j, :mrows, half:] = imag
        mix[j, mrows:, :half] = -imag
        mix[j, mrows:, half:] = real

    def plain(i, j, w):
        xacc[j] += jnp.dot(mix[i], w, preferred_element_type=F32)

    def adjoint(i, j, w):
        p = nt(lhs[j], w)
        xacc[i, :mrows, lanes] += p[:mrows, :half] - p[mrows:, half:]
        xacc[i, mrows:, lanes] -= p[:mrows, half:] + p[mrows:, :half]

    def block(i, j):
        return wall[i, j].reshape(2 * half, 2 * half)

    plain(z, z, block(z, z))
    for n in range(1, rows):
        j = (z + n) % rows
        plain(z, j, block(z, j))
        adjoint(z, j, block(z, j))

    stacked(vbuf, vr, vl)

    nsq, noth = len(squares[0]), len(others[0])
    for n in range(max(nsq, noth)):
        if n < nsq:
            i = pick(z, [s[n][0] for s in squares])
            pltpu.make_async_copy(packed.at[i], packed.at[i], zr.at[i, i]).wait()
            both = packed[i].astype(F32)
            real = jnp.where(at_col >= at_row, both, 0.0).astype(BF16)
            above = jnp.where(at_col > at_row, both, 0.0).astype(BF16)
            imag = jnp.where(at_col < at_row, both, 0.0).astype(BF16)
            plain(i, i, jnp.concatenate([real, imag], 0))
            adjoint(i, i, jnp.concatenate([above, imag], 0))
        if n < noth:
            i = pick(z, [s[n][0] for s in others])
            j = pick(z, [s[n][1] for s in others])
            pltpu.make_async_copy(wall.at[i, j], wall.at[i, j], zr.at[i, j]).wait()
            plain(i, j, block(i, j))
            adjoint(i, j, block(i, j))

    with_real = jnp.zeros((2 * mrows, mrows), F32)
    with_imag = jnp.zeros((2 * mrows, mrows), F32)
    for j in range(rows):
        total = xacc[j]
        high = total.astype(BF16)
        low = (total - high.astype(F32)).astype(BF16)
        vreal, vimag = vl[j, :mrows], vl[j, mrows:]
        with_real += nt(high, vreal) + nt(low, vreal)
        with_imag += nt(high, vimag) + nt(low, vimag)
    kreal = with_real[:mrows] - with_imag[mrows:]
    kimag = with_imag[:mrows] + with_real[mrows:]

    width = npair * npair
    row = lax.broadcasted_iota(jnp.int32, (mrows, mrows), 0)
    col = lax.broadcasted_iota(jnp.int32, (mrows, mrows), 1)
    same_k = lax.div(row, npair) == lax.div(col, npair)
    vrow = lax.broadcasted_iota(jnp.int32, (mrows, width), 0)
    lane = lax.broadcasted_iota(jnp.int32, (mrows, width), 1)
    spread = jnp.where(lax.rem(vrow, npair) == lax.rem(lane, npair), 1.0, 0.0).astype(F32)
    same_a = lax.rem(vrow, npair) == lax.div(lane, npair)
    kgrid = mrows // npair
    for part, value in enumerate((kreal, kimag)):
        wide = jnp.dot(jnp.where(same_k, value, 0.0), spread, precision=HIGHEST, preferred_element_type=F32)
        wide = jnp.where(same_a, wide, 0.0).reshape(kgrid, npair, width)
        kown[pl.ds(part * kgrid, kgrid), :] = wide.sum(1)

    pair_sum = remote(kown, ksib, ks, kr, dev(z, y, x, 1 - h))
    pair_sum.start()
    pair_sum.wait()
    total = kown[...] + ksib[...]
    share = kstage.shape[2]
    for n in range(kstage.shape[0]):
        kstage[n] = total[:, n * share:(n + 1) * share]

    def out_copies():
        n = 0
        for dz in range(rows):
            for dy in range(2):
                for dx in range(2):
                    if dz or dy or dx:
                        zz, yy, xx = (z + dz) % rows, (y + dy) % 2, (x + dx) % 2
                        yield remote(
                            kstage.at[2 * xx + h], kall.at[mine, z], os.at[n], orr.at[mine, z], dev(zz, yy, xx, h)
                        )
                        n += 1

    for copy in out_copies():
        copy.start()
    kall[mine, z] = kstage[g]
    for dz in range(rows):
        for dy in range(2):
            for dx in range(2):
                if dz or dy or dx:
                    zz = (z + dz) % rows
                    qq = 2 * ((x + dx) % 2) + (y + dy) % 2
                    pltpu.make_async_copy(kall.at[qq, zz], kall.at[qq, zz], orr.at[qq, zz]).wait()

    outs = 2 * kpd
    o = lax.broadcasted_iota(jnp.int32, (outs, rows * 2 * kgrid), 0)
    r = lax.broadcasted_iota(jnp.int32, (outs, rows * 2 * kgrid), 1)
    k_here = y * kpd + lax.div(o, 2)
    part_at = lax.rem(o, 2) * kgrid
    ahead = jnp.where(r == z * 2 * kgrid + part_at + k_here, 1.0, 0.0).astype(F32)
    for q in range(kall.shape[0]):
        table = kall[q].reshape(rows * 2 * kgrid, share)
        corner = kp_ref[q, 0]
        row_step = lax.div(corner, kgrid)
        col_step = lax.rem(corner, kgrid)
        src_row = lax.rem(z - row_step + rows, rows)
        src_col = lax.rem(k_here - col_step + kgrid, kgrid)
        behind = jnp.where(r == src_row * 2 * kgrid + part_at + src_col, 1.0, 0.0).astype(F32)
        for ref, choice in ((f_ref, ahead), (b_ref, behind)):
            chosen = jnp.dot(choice, table, precision=HIGHEST, preferred_element_type=F32)
            for t in range(kpd):
                ref[q, t] = chosen[2 * t:2 * t + 2]

    for n in range(3):
        w_copy(n).wait_send()
        pair_copy(c_ref, cbuf, cs, cr, n).wait_send()
        pair_copy(v_ref, vbuf, vs, vr, n).wait_send()

    @pl.when(h != y)
    def _():
        w_copy(3).wait_send()

    for src in range(rows):
        @pl.when(z == src)
        def _():
            for copy in z_copies(src):
                copy.wait_send()

    for buf, rsem, fsem in ((cbuf, cr, cfs), (vbuf, vr, vfs)):
        for dy in range(2):
            for dx in range(2):
                hand_on(buf, fsem, rsem, (y + dy) % 2, (x + dx) % 2).wait_send()
    for copy in out_copies():
        copy.wait_send()


def exchanged(cond_pairs, val_pairs, screened, k_plus):
    nq, kpd, _, npair, cols = cond_pairs.shape
    half = screened.shape[2]
    rows = lax.axis_size("ka") // 2
    ga = lax.axis_size("ga")
    mrows = 2 * kpd * npair
    width = npair * npair
    share = width // ga
    dma = pltpu.SemaphoreType.DMA
    out = jax.ShapeDtypeStruct((nq, kpd, 2, share), F32)
    squares, others = block_plan(rows)
    most = max(
        sum(i == src for d in range(rows) for i, _ in squares[d] + others[d]) for src in range(rows)
    )
    return pl.pallas_call(
        functools.partial(kernel, rows),
        out_shape=(out, out),
        in_specs=[pl.BlockSpec(memory_space=pltpu.HBM)] * 3 + [pl.BlockSpec(memory_space=pltpu.SMEM)],
        out_specs=[pl.BlockSpec(memory_space=pltpu.VMEM)] * 2,
        scratch_shapes=[
            pltpu.VMEM((rows, rows, 2, half, cols), BF16),
            pltpu.VMEM((rows, half, cols), BF16),
            pltpu.VMEM((2, ga, kpd, 2, npair, cols), BF16),
            pltpu.VMEM((2, ga, kpd, 2, npair, cols), BF16),
            pltpu.VMEM((ga, 2 * mrows, cols), BF16),
            pltpu.VMEM((ga, 2 * mrows, cols), BF16),
            pltpu.VMEM((ga, 2 * mrows, cols), BF16),
            pltpu.VMEM((ga, 2 * mrows, cols), F32),
            pltpu.VMEM((4 * kpd, width), F32),
            pltpu.VMEM((4 * kpd, width), F32),
            pltpu.VMEM((ga, 4 * kpd, share), F32),
            pltpu.VMEM((nq, rows, 4 * kpd, share), F32),
            dma((4,)), dma((ga,)),
            dma((3,)), dma((2, ga)),
            dma((3,)), dma((2, ga)),
            dma((2, 2)), dma((2, 2)),
            dma((most,)), dma((rows, rows)),
            dma, dma,
            dma((4 * rows - 1,)), dma((nq, rows)),
        ],
        compiler_params=pltpu.CompilerParams(
            collective_id=0, has_side_effects=True, vmem_limit_bytes=64 * 1024 * 1024
        ),
    )(cond_pairs, val_pairs, screened, k_plus)


NG = 1024
Q = 4
npair = 16
npair = 16


def passed_along(block, axis, distance):
    devices = range(lax.axis_size(axis))
    route = [((i - distance) % len(devices), i) for i in devices]
    return lax.ppermute(block, axis, route)


def swapped(shard, axis, bit):
    return lax.ppermute(shard, axis, [(i, i ^ 1 << bit) for i in range(lax.axis_size(axis))])


def screen_fold(left_real, left_imag, piece):
    real_next = jnp.dot(left_real, piece[0], preferred_element_type=jnp.float32) + jnp.dot(
        left_imag, piece[1], preferred_element_type=jnp.float32
    )
    imag_next = jnp.dot(left_real, piece[1], preferred_element_type=jnp.float32) - jnp.dot(
        left_imag, piece[0], preferred_element_type=jnp.float32
    )
    return (real_next, imag_next)


def pair_contract(left, right):
    return jnp.einsum("kag,kbg->kab", left, right, preferred_element_type=jnp.float32)


def local(cond_pairs, val_pairs, screened, k_plus):
    nq, local_k, _, npair, own = cond_pairs.shape
    ng = own * lax.axis_size("ga")
    columns = screened.shape[3]
    grid_y = 2 * local_k
    forward = []
    for q_index in range(nq):
        cond_full = lax.all_gather(cond_pairs[q_index], "ga", axis=3, tiled=True)
        left_real = cond_full[:, 0].reshape(local_k * npair, ng)
        left_imag = cond_full[:, 1].reshape(local_k * npair, ng)
        real_x, imag_x = screen_fold(
            left_real, left_imag, lax.all_gather(screened[q_index], "ka", axis=1, tiled=True)
        )
        real_b = real_x.astype(jnp.bfloat16).reshape(local_k, npair, columns)
        imag_b = imag_x.astype(jnp.bfloat16).reshape(local_k, npair, columns)
        val_real = val_pairs[q_index][:, 0]
        val_imag = val_pairs[q_index][:, 1]
        kernel_real = pair_contract(real_b, val_real) - pair_contract(imag_b, val_imag)
        kernel_imag = pair_contract(real_b, val_imag) + pair_contract(imag_b, val_real)
        forward.append(jnp.stack([kernel_real, kernel_imag], 1).reshape(local_k, 2, npair * npair))
    partial_value = jnp.stack(forward, 0)
    total = lax.psum(partial_value, "ga")
    width = total.shape[3] // lax.axis_size("ga")
    kernel_share = lax.dynamic_slice_in_dim(total, lax.axis_index("ga") * width, width, 3)
    count = lax.axis_size("ka")
    corner = k_plus[:, 0]
    row_step = corner // grid_y
    col_step = corner % grid_y
    hop_length = 2 * row_step % count
    moved = kernel_share
    nbits = count.bit_length() - 1
    for bit_number in range(1, nbits):
        arrived = passed_along(moved, "ka", 1 << bit_number)
        taken = hop_length // (1 << bit_number) % 2 == 1
        moved = jnp.where(taken[:, None, None, None], arrived, moved)
    partner = swapped(moved, "ka", 0)
    half_index = lax.axis_index("ka") % 2
    whole_row = jnp.where(
        half_index == 0, jnp.concatenate([moved, partner], 1), jnp.concatenate([partner, moved], 1)
    )
    doubled = jnp.concatenate([whole_row, whole_row], 1)
    backs = []
    for q_index in range(nq):
        begin = (half_index * local_k - col_step[q_index] + grid_y) % grid_y
        backs.append(lax.dynamic_slice_in_dim(doubled[q_index], begin, local_k, 0))
    kernel_back = jnp.stack(backs, 0)
    return (kernel_share, kernel_back)


def solution(mesh):
    in_specs = (
        P(None, "ka", None, None, "ga"),
        P(None, "ka", None, None, "ga"),
        P(None, None, "ka", "ga"),
        P(),
    )
    out_specs = (P(None, "ka", None, "ga"), P(None, "ka", None, "ga"))
    square = mesh.shape["ga"] == 4 and mesh.shape["ka"] == 2 * mesh.shape["ga"]
    body = exchanged if square else local
    return jax.shard_map(body, mesh=mesh, in_specs=in_specs, out_specs=out_specs, check_vma=False)
```

```python
import functools

import jax
import jax.numpy as jnp
from jax import lax
from jax.experimental import pallas as pl
from jax.experimental.pallas import tpu as pltpu
from jax.sharding import PartitionSpec as P

MESH = pl.DeviceIdType.MESH
HIGHEST = lax.Precision.HIGHEST
F32 = jnp.float32
BF16 = jnp.bfloat16


def nearest_source(pair, dest):
    i, j = pair
    if abs(i - dest) == abs(j - dest):
        return i if i == 0 else j
    return i if abs(i - dest) < abs(j - dest) else j


def block_plan(rows):
    squares, others = [], []
    for dest in range(rows):
        squares.append(sorted(((i, i) for i in range(rows) if i != dest), key=lambda b: abs(b[0] - dest)))
        blocks = []
        for i in range(rows):
            for j in range(i + 1, rows):
                if dest not in (i, j):
                    src = nearest_source((i, j), dest)
                    blocks.append((src, i + j - src))
        others.append(sorted(blocks, key=lambda b: abs(b[0] - dest)))
    return squares, others


def pick(index, values):
    out = jnp.int32(values[0])
    for n in range(1, len(values)):
        out = jnp.where(index == n, jnp.int32(values[n]), out)
    return out


def nt(a, b):
    return lax.dot_general(a, b, (((1,), (1,)), ((), ())), preferred_element_type=F32)


def kernel(
    rows, c_ref, v_ref, w_ref, all_ref,
    wall, packed, cbuf, vbuf, lhs, mix, vl, xacc, kown, ksib, kstage, kall,
    w1s, w1r, cs, cr, vs, vr, cfs, vfs, zs, zr, ks, kr, os, orr,
):
    kpd, npair = cbuf.shape[2], cbuf.shape[4]
    half = wall.shape[3]
    mrows = 2 * kpd * npair
    ka, g = lax.axis_index("ka"), lax.axis_index("ga")
    z, y = ka // 2, ka % 2
    x, h = g // 2, g % 2
    mine = 2 * x + y

    def dev(zz, yy, xx, hh):
        return (2 * zz + yy, 2 * xx + hh)

    def remote(src, dst, ssem, rsem, target):
        return pltpu.make_async_remote_copy(
            src_ref=src, dst_ref=dst, send_sem=ssem, recv_sem=rsem, device_id=target, device_id_type=MESH
        )

    barrier = pltpu.get_barrier_semaphore()
    count = 0
    for dz in range(rows):
        for dy in range(2):
            for dx in range(2):
                for dh in range(2):
                    if (dz and dh) or not (dz or dy or dx or dh):
                        continue
                    pl.semaphore_signal(
                        barrier, inc=1,
                        device_id=dev((z + dz) % rows, (y + dy) % 2, (x + dx) % 2, (h + dh) % 2),
                        device_id_type=MESH,
                    )
                    count += 1
    pl.semaphore_wait(barrier, count)

    steps = [(1, 1), (1, 0), (0, 1), (0, 0)]

    def w_copy(n, part):
        dy, dx = steps[n]
        qy, qx = (y + dy) % 2, (x + dx) % 2
        return remote(
            w_ref.at[2 * qx + qy, part], wall.at[z, g, part], w1s.at[n, part], w1r.at[g, part], dev(z, qy, qx, y)
        )

    for part in range(2):
        for n in range(3):
            w_copy(n, part).start()

        @pl.when(h == y)
        def _():
            pltpu.make_async_copy(w_ref.at[mine, part], wall.at[z, g, part], w1r.at[g, part]).start()

        @pl.when(h != y)
        def _():
            w_copy(3, part).start()

    def pair_copy(ref, buf, ssem, rsem, n):
        dy, dx = steps[n]
        qy, qx = (y + dy) % 2, (x + dx) % 2
        return remote(ref.at[2 * qx + qy], buf.at[y, g], ssem.at[n], rsem.at[y, g], dev(z, qy, qx, h))

    xacc[...] = jnp.zeros_like(xacc)

    for ref, buf, ssem, rsem in ((c_ref, cbuf, cs, cr), (v_ref, vbuf, vs, vr)):
        for n in range(3):
            pair_copy(ref, buf, ssem, rsem, n).start()
        pltpu.make_async_copy(ref.at[mine], buf.at[y, g], rsem.at[y, g]).start()

    squares, others = block_plan(rows)
    sends = [[] for _ in range(rows)]
    for dest in range(rows):
        for i, j in squares[dest] + others[dest]:
            sends[i].append((dest, j))

    at_row = h * half + lax.broadcasted_iota(jnp.int32, (half, 2 * half), 0)
    at_col = lax.broadcasted_iota(jnp.int32, (half, 2 * half), 1)

    def z_copies(src, which=None):
        order = sorted(sends[src], key=lambda s: (s[1], -abs(s[0] - src)))
        for n, (dest, j) in enumerate(order):
            for part in range(2):
                if which is not None and (j, part) != which or j == src and part == 0:
                    continue
                ref = packed.at[src] if j == src else wall.at[src, j, part]
                yield remote(ref, ref, zs.at[n, part], zr.at[src, j, part], dev(dest, y, x, h))

    for part in range(2):
        for j in range(rows):
            pltpu.make_async_copy(wall.at[z, j, part], wall.at[z, j, part], w1r.at[j, part]).wait()
            for src in range(rows):
                @pl.when(z == src)
                def _():
                    if j == src and part == 1:
                        upper = at_col >= at_row
                        packed[src] = jnp.where(
                            upper, wall[src, src, 0].astype(F32), wall[src, src, 1].astype(F32)
                        ).astype(BF16)
                    for copy in z_copies(src, (j, part)):
                        copy.start()

    def hand_on(buf, ssem, rsem, yy, xx):
        slot = buf.at[yy, 2 * xx + h]
        return remote(slot, slot, ssem.at[yy, xx], rsem.at[yy, 2 * xx + h], dev(z, y, x, 1 - h))

    def arrived(buf, rsem, yy, j):
        pltpu.make_async_copy(buf.at[yy, j], buf.at[yy, j], rsem.at[yy, j]).wait()

    for buf, rsem, fsem in ((cbuf, cr, cfs), (vbuf, vr, vfs)):
        for dy in range(2):
            for dx in range(2):
                yy, xx = (y + dy) % 2, (x + dx) % 2
                arrived(buf, rsem, yy, 2 * xx + h)
                hand_on(buf, fsem, rsem, yy, xx).start()

    def stacked(buf, rsem, out):
        for yy in range(2):
            for xx in range(2):
                arrived(buf, rsem, yy, 2 * xx + 1 - h)
        for j in range(rows):
            for yy in range(2):
                for part in range(2):
                    block = buf[yy, j, :, part].reshape(kpd * npair, 2 * half)
                    out[j, pl.ds((2 * part + yy) * kpd * npair, kpd * npair), :] = block

    lanes = pl.ds(pl.multiple_of(h * half, half), half)
    stacked(cbuf, cr, lhs)
    for j in range(rows):
        both = lhs[j, :, lanes]
        real, imag = both[:mrows], both[mrows:]
        mix[j, :mrows, :half] = real
        mix[j, :mrows, half:] = imag
        mix[j, mrows:, :half] = -imag
        mix[j, mrows:, half:] = real

    def plain(i, j, w):
        xacc[j] += jnp.dot(mix[i], w, preferred_element_type=F32)

    def adjoint(i, j, w):
        p = nt(lhs[j], w)
        xacc[i, :mrows, lanes] += p[:mrows, :half] - p[mrows:, half:]
        xacc[i, mrows:, lanes] -= p[:mrows, half:] + p[mrows:, :half]

    def block(i, j):
        return wall[i, j].reshape(2 * half, 2 * half)

    plain(z, z, block(z, z))
    for n in range(1, rows):
        j = (z + n) % rows
        plain(z, j, block(z, j))
        adjoint(z, j, block(z, j))

    stacked(vbuf, vr, vl)

    nsq, noth = len(squares[0]), len(others[0])
    for n in range(max(nsq, noth)):
        if n < noth:
            i = pick(z, [s[n][0] for s in others])
            j = pick(z, [s[n][1] for s in others])
            for part in range(2):
                pltpu.make_async_copy(wall.at[i, j, part], wall.at[i, j, part], zr.at[i, j, part]).wait()
            plain(i, j, block(i, j))
            adjoint(i, j, block(i, j))
        if n < nsq:
            i = pick(z, [s[n][0] for s in squares])
            pltpu.make_async_copy(packed.at[i], packed.at[i], zr.at[i, i, 1]).wait()
            both = packed[i].astype(F32)
            real = jnp.where(at_col >= at_row, both, 0.0).astype(BF16)
            above = jnp.where(at_col > at_row, both, 0.0).astype(BF16)
            imag = jnp.where(at_col < at_row, both, 0.0).astype(BF16)
            plain(i, i, jnp.concatenate([real, imag], 0))
            adjoint(i, i, jnp.concatenate([above, imag], 0))

    with_real = jnp.zeros((2 * mrows, mrows), F32)
    with_imag = jnp.zeros((2 * mrows, mrows), F32)
    for j in range(rows):
        total = xacc[j]
        high = total.astype(BF16)
        low = (total - high.astype(F32)).astype(BF16)
        vreal, vimag = vl[j, :mrows], vl[j, mrows:]
        with_real += nt(high, vreal) + nt(low, vreal)
        with_imag += nt(high, vimag) + nt(low, vimag)
    kreal = with_real[:mrows] - with_imag[mrows:]
    kimag = with_imag[:mrows] + with_real[mrows:]

    width = npair * npair
    row = lax.broadcasted_iota(jnp.int32, (mrows, mrows), 0)
    col = lax.broadcasted_iota(jnp.int32, (mrows, mrows), 1)
    same_k = lax.div(row, npair) == lax.div(col, npair)
    vrow = lax.broadcasted_iota(jnp.int32, (mrows, width), 0)
    lane = lax.broadcasted_iota(jnp.int32, (mrows, width), 1)
    spread = jnp.where(lax.rem(vrow, npair) == lax.rem(lane, npair), 1.0, 0.0).astype(F32)
    same_a = lax.rem(vrow, npair) == lax.div(lane, npair)
    kgrid = mrows // npair
    for part, value in enumerate((kreal, kimag)):
        wide = jnp.dot(jnp.where(same_k, value, 0.0), spread, precision=HIGHEST, preferred_element_type=F32)
        wide = jnp.where(same_a, wide, 0.0).reshape(kgrid, npair, width)
        kown[pl.ds(part * kgrid, kgrid), :] = wide.sum(1)

    pair_sum = remote(kown, ksib, ks, kr, dev(z, y, x, 1 - h))
    pair_sum.start()
    pair_sum.wait()
    total = kown[...] + ksib[...]
    share = kstage.shape[2]
    for n in range(kstage.shape[0]):
        kstage[n] = total[:, n * share:(n + 1) * share]

    def out_copies():
        n = 0
        for dz in range(rows):
            for dy in range(2):
                for dx in range(2):
                    if dz or dy or dx:
                        zz, yy, xx = (z + dz) % rows, (y + dy) % 2, (x + dx) % 2
                        yield remote(
                            kstage.at[2 * xx + h], kall.at[mine, z], os.at[n], orr.at[mine, z], dev(zz, yy, xx, h)
                        )
                        n += 1

    for copy in out_copies():
        copy.start()
    kall[mine, z] = kstage[g]
    for dz in range(rows):
        for dy in range(2):
            for dx in range(2):
                if dz or dy or dx:
                    zz = (z + dz) % rows
                    qq = 2 * ((x + dx) % 2) + (y + dy) % 2
                    pltpu.make_async_copy(kall.at[qq, zz], kall.at[qq, zz], orr.at[qq, zz]).wait()

    all_ref[...] = kall[...]

    for n in range(3):
        for part in range(2):
            w_copy(n, part).wait_send()
        pair_copy(c_ref, cbuf, cs, cr, n).wait_send()
        pair_copy(v_ref, vbuf, vs, vr, n).wait_send()

    @pl.when(h != y)
    def _():
        for part in range(2):
            w_copy(3, part).wait_send()

    for src in range(rows):
        @pl.when(z == src)
        def _():
            for copy in z_copies(src):
                copy.wait_send()

    for buf, rsem, fsem in ((cbuf, cr, cfs), (vbuf, vr, vfs)):
        for dy in range(2):
            for dx in range(2):
                hand_on(buf, fsem, rsem, (y + dy) % 2, (x + dx) % 2).wait_send()
    for copy in out_copies():
        copy.wait_send()


def choose(rows, kp_ref, kall, f_ref, b_ref):
    kpd, share = f_ref.shape[1], f_ref.shape[3]
    kgrid = 2 * kpd
    ka = lax.axis_index("ka")
    z, y = ka // 2, ka % 2
    outs = 2 * kpd
    o = lax.broadcasted_iota(jnp.int32, (outs, rows * 2 * kgrid), 0)
    r = lax.broadcasted_iota(jnp.int32, (outs, rows * 2 * kgrid), 1)
    k_here = y * kpd + lax.div(o, 2)
    part_at = lax.rem(o, 2) * kgrid
    ahead = jnp.where(r == z * 2 * kgrid + part_at + k_here, 1.0, 0.0).astype(F32)
    for q in range(kall.shape[0]):
        table = kall[q].reshape(rows * 2 * kgrid, share)
        corner = kp_ref[q, 0]
        row_step = lax.div(corner, kgrid)
        col_step = lax.rem(corner, kgrid)
        src_row = lax.rem(z - row_step + rows, rows)
        src_col = lax.rem(k_here - col_step + kgrid, kgrid)
        behind = jnp.where(r == src_row * 2 * kgrid + part_at + src_col, 1.0, 0.0).astype(F32)
        for ref, choice in ((f_ref, ahead), (b_ref, behind)):
            chosen = jnp.dot(choice, table, precision=HIGHEST, preferred_element_type=F32)
            for t in range(kpd):
                ref[q, t] = chosen[2 * t:2 * t + 2]


def exchanged(cond_pairs, val_pairs, screened, k_plus):
    nq, kpd, _, npair, cols = cond_pairs.shape
    half = screened.shape[2]
    rows = lax.axis_size("ka") // 2
    ga = lax.axis_size("ga")
    mrows = 2 * kpd * npair
    width = npair * npair
    share = width // ga
    dma = pltpu.SemaphoreType.DMA
    out = jax.ShapeDtypeStruct((nq, kpd, 2, share), F32)
    squares, others = block_plan(rows)
    most = max(
        sum(i == src for d in range(rows) for i, _ in squares[d] + others[d]) for src in range(rows)
    )
    blocks = pl.pallas_call(
        functools.partial(kernel, rows),
        out_shape=jax.ShapeDtypeStruct((nq, rows, 4 * kpd, share), F32),
        in_specs=[pl.BlockSpec(memory_space=pltpu.HBM)] * 3,
        out_specs=pl.BlockSpec(memory_space=pltpu.VMEM),
        scratch_shapes=[
            pltpu.VMEM((rows, rows, 2, half, cols), BF16),
            pltpu.VMEM((rows, half, cols), BF16),
            pltpu.VMEM((2, ga, kpd, 2, npair, cols), BF16),
            pltpu.VMEM((2, ga, kpd, 2, npair, cols), BF16),
            pltpu.VMEM((ga, 2 * mrows, cols), BF16),
            pltpu.VMEM((ga, 2 * mrows, cols), BF16),
            pltpu.VMEM((ga, 2 * mrows, cols), BF16),
            pltpu.VMEM((ga, 2 * mrows, cols), F32),
            pltpu.VMEM((4 * kpd, width), F32),
            pltpu.VMEM((4 * kpd, width), F32),
            pltpu.VMEM((ga, 4 * kpd, share), F32),
            pltpu.VMEM((nq, rows, 4 * kpd, share), F32),
            dma((4, 2)), dma((ga, 2)),
            dma((3,)), dma((2, ga)),
            dma((3,)), dma((2, ga)),
            dma((2, 2)), dma((2, 2)),
            dma((most, 2)), dma((rows, rows, 2)),
            dma, dma,
            dma((4 * rows - 1,)), dma((nq, rows)),
        ],
        compiler_params=pltpu.CompilerParams(
            collective_id=0, has_side_effects=True, vmem_limit_bytes=64 * 1024 * 1024 - 320 * 1024
        ),
    )(cond_pairs, val_pairs, screened)
    return pl.pallas_call(
        functools.partial(choose, rows),
        out_shape=(out, out),
        in_specs=[pl.BlockSpec(memory_space=pltpu.SMEM), pl.BlockSpec(memory_space=pltpu.VMEM)],
        out_specs=[pl.BlockSpec(memory_space=pltpu.VMEM)] * 2,
    )(k_plus, blocks)


NG = 1024
Q = 4
npair = 16
npair = 16


def passed_along(block, axis, distance):
    devices = range(lax.axis_size(axis))
    route = [((i - distance) % len(devices), i) for i in devices]
    return lax.ppermute(block, axis, route)


def swapped(shard, axis, bit):
    return lax.ppermute(shard, axis, [(i, i ^ 1 << bit) for i in range(lax.axis_size(axis))])


def screen_fold(left_real, left_imag, piece):
    real_next = jnp.dot(left_real, piece[0], preferred_element_type=jnp.float32) + jnp.dot(
        left_imag, piece[1], preferred_element_type=jnp.float32
    )
    imag_next = jnp.dot(left_real, piece[1], preferred_element_type=jnp.float32) - jnp.dot(
        left_imag, piece[0], preferred_element_type=jnp.float32
    )
    return (real_next, imag_next)


def pair_contract(left, right):
    return jnp.einsum("kag,kbg->kab", left, right, preferred_element_type=jnp.float32)


def local(cond_pairs, val_pairs, screened, k_plus):
    nq, local_k, _, npair, own = cond_pairs.shape
    ng = own * lax.axis_size("ga")
    columns = screened.shape[3]
    grid_y = 2 * local_k
    forward = []
    for q_index in range(nq):
        cond_full = lax.all_gather(cond_pairs[q_index], "ga", axis=3, tiled=True)
        left_real = cond_full[:, 0].reshape(local_k * npair, ng)
        left_imag = cond_full[:, 1].reshape(local_k * npair, ng)
        real_x, imag_x = screen_fold(
            left_real, left_imag, lax.all_gather(screened[q_index], "ka", axis=1, tiled=True)
        )
        real_b = real_x.astype(jnp.bfloat16).reshape(local_k, npair, columns)
        imag_b = imag_x.astype(jnp.bfloat16).reshape(local_k, npair, columns)
        val_real = val_pairs[q_index][:, 0]
        val_imag = val_pairs[q_index][:, 1]
        kernel_real = pair_contract(real_b, val_real) - pair_contract(imag_b, val_imag)
        kernel_imag = pair_contract(real_b, val_imag) + pair_contract(imag_b, val_real)
        forward.append(jnp.stack([kernel_real, kernel_imag], 1).reshape(local_k, 2, npair * npair))
    partial_value = jnp.stack(forward, 0)
    total = lax.psum(partial_value, "ga")
    width = total.shape[3] // lax.axis_size("ga")
    kernel_share = lax.dynamic_slice_in_dim(total, lax.axis_index("ga") * width, width, 3)
    count = lax.axis_size("ka")
    corner = k_plus[:, 0]
    row_step = corner // grid_y
    col_step = corner % grid_y
    hop_length = 2 * row_step % count
    moved = kernel_share
    nbits = count.bit_length() - 1
    for bit_number in range(1, nbits):
        arrived = passed_along(moved, "ka", 1 << bit_number)
        taken = hop_length // (1 << bit_number) % 2 == 1
        moved = jnp.where(taken[:, None, None, None], arrived, moved)
    partner = swapped(moved, "ka", 0)
    half_index = lax.axis_index("ka") % 2
    whole_row = jnp.where(
        half_index == 0, jnp.concatenate([moved, partner], 1), jnp.concatenate([partner, moved], 1)
    )
    doubled = jnp.concatenate([whole_row, whole_row], 1)
    backs = []
    for q_index in range(nq):
        begin = (half_index * local_k - col_step[q_index] + grid_y) % grid_y
        backs.append(lax.dynamic_slice_in_dim(doubled[q_index], begin, local_k, 0))
    kernel_back = jnp.stack(backs, 0)
    return (kernel_share, kernel_back)


def solution(mesh):
    in_specs = (
        P(None, "ka", None, None, "ga"),
        P(None, "ka", None, None, "ga"),
        P(None, None, "ka", "ga"),
        P(),
    )
    out_specs = (P(None, "ka", None, "ga"), P(None, "ka", None, "ga"))
    square = mesh.shape["ga"] == 4 and mesh.shape["ka"] == 2 * mesh.shape["ga"]
    body = exchanged if square else local
    return jax.shard_map(body, mesh=mesh, in_specs=in_specs, out_specs=out_specs, check_vma=False)
```

```python
import functools

import jax
import jax.numpy as jnp
from jax import lax
from jax.experimental import pallas as pl
from jax.experimental.pallas import tpu as pltpu
from jax.sharding import PartitionSpec as P

MESH = pl.DeviceIdType.MESH
F32 = jnp.float32
BF16 = jnp.bfloat16


def nearest_source(pair, dest):
    i, j = pair
    if abs(i - dest) == abs(j - dest):
        return i if i == 0 else j
    return i if abs(i - dest) < abs(j - dest) else j


def block_plan(rows):
    squares, others = [], []
    for dest in range(rows):
        squares.append(sorted(((i, i) for i in range(rows) if i != dest), key=lambda b: abs(b[0] - dest)))
        blocks = []
        for i in range(rows):
            for j in range(i + 1, rows):
                if dest not in (i, j):
                    src = nearest_source((i, j), dest)
                    blocks.append((src, i + j - src))
        others.append(sorted(blocks, key=lambda b: abs(b[0] - dest)))
    return squares, others


def pick(index, values):
    out = jnp.int32(values[0])
    for n in range(1, len(values)):
        out = jnp.where(index == n, jnp.int32(values[n]), out)
    return out


def nt(a, b):
    return lax.dot_general(a, b, (((1,), (1,)), ((), ())), preferred_element_type=F32)


def thirds(value):
    high = value.astype(BF16)
    rest = value - high.astype(F32)
    middle = rest.astype(BF16)
    return high, middle, (rest - middle.astype(F32)).astype(BF16)


def kernel(
    rows, c_ref, v_ref, w_ref, all_ref,
    wall, packed, cbuf, vbuf, lhs, mix, vl, xacc, kown, ksib, kstage, kall,
    w1s, w1r, cs, cr, vs, vr, cfs, vfs, zs, zr, ks, kr, os, orr,
):
    kpd, npair = cbuf.shape[2], cbuf.shape[4]
    half = wall.shape[3]
    mrows = 2 * kpd * npair
    ka, g = lax.axis_index("ka"), lax.axis_index("ga")
    z, y = ka // 2, ka % 2
    x, h = g // 2, g % 2
    mine = 2 * x + y

    def dev(zz, yy, xx, hh):
        return (2 * zz + yy, 2 * xx + hh)

    def remote(src, dst, ssem, rsem, target):
        return pltpu.make_async_remote_copy(
            src_ref=src, dst_ref=dst, send_sem=ssem, recv_sem=rsem, device_id=target, device_id_type=MESH
        )

    barrier = pltpu.get_barrier_semaphore()
    count = 0
    for dz in range(rows):
        for dy in range(2):
            for dx in range(2):
                for dh in range(2):
                    if (dz and dh) or not (dz or dy or dx or dh):
                        continue
                    pl.semaphore_signal(
                        barrier, inc=1,
                        device_id=dev((z + dz) % rows, (y + dy) % 2, (x + dx) % 2, (h + dh) % 2),
                        device_id_type=MESH,
                    )
                    count += 1
    pl.semaphore_wait(barrier, count)

    steps = [(1, 1), (1, 0), (0, 1), (0, 0)]

    def w_copy(n, part):
        dy, dx = steps[n]
        qy, qx = (y + dy) % 2, (x + dx) % 2
        return remote(
            w_ref.at[2 * qx + qy, part], wall.at[z, g, part], w1s.at[n, part], w1r.at[g, part], dev(z, qy, qx, y)
        )

    for part in range(2):
        for n in range(3):
            w_copy(n, part).start()

        @pl.when(h == y)
        def _():
            pltpu.make_async_copy(w_ref.at[mine, part], wall.at[z, g, part], w1r.at[g, part]).start()

        @pl.when(h != y)
        def _():
            w_copy(3, part).start()

    def pair_copy(ref, buf, ssem, rsem, n):
        dy, dx = steps[n]
        qy, qx = (y + dy) % 2, (x + dx) % 2
        return remote(ref.at[2 * qx + qy], buf.at[y, g], ssem.at[n], rsem.at[y, g], dev(z, qy, qx, h))

    xacc[...] = jnp.zeros_like(xacc)

    for ref, buf, ssem, rsem in ((c_ref, cbuf, cs, cr), (v_ref, vbuf, vs, vr)):
        for n in range(3):
            pair_copy(ref, buf, ssem, rsem, n).start()
        pltpu.make_async_copy(ref.at[mine], buf.at[y, g], rsem.at[y, g]).start()

    squares, others = block_plan(rows)
    sends = [[] for _ in range(rows)]
    for dest in range(rows):
        for i, j in squares[dest] + others[dest]:
            sends[i].append((dest, j))

    at_row = h * half + lax.broadcasted_iota(jnp.int32, (half, 2 * half), 0)
    at_col = lax.broadcasted_iota(jnp.int32, (half, 2 * half), 1)

    def z_copies(src, which=None):
        order = sorted(sends[src], key=lambda s: (s[1], -abs(s[0] - src)))
        for n, (dest, j) in enumerate(order):
            for part in range(2):
                if which is not None and (j, part) != which or j == src and part == 0:
                    continue
                ref = packed.at[src] if j == src else wall.at[src, j, part]
                yield remote(ref, ref, zs.at[n, part], zr.at[src, j, part], dev(dest, y, x, h))

    for part in range(2):
        for j in range(rows):
            pltpu.make_async_copy(wall.at[z, j, part], wall.at[z, j, part], w1r.at[j, part]).wait()
            for src in range(rows):
                @pl.when(z == src)
                def _():
                    if j == src and part == 1:
                        upper = at_col >= at_row
                        packed[src] = jnp.where(
                            upper, wall[src, src, 0].astype(F32), wall[src, src, 1].astype(F32)
                        ).astype(BF16)
                    for copy in z_copies(src, (j, part)):
                        copy.start()

    def hand_on(buf, ssem, rsem, yy, xx):
        slot = buf.at[yy, 2 * xx + h]
        return remote(slot, slot, ssem.at[yy, xx], rsem.at[yy, 2 * xx + h], dev(z, y, x, 1 - h))

    def arrived(buf, rsem, yy, j):
        pltpu.make_async_copy(buf.at[yy, j], buf.at[yy, j], rsem.at[yy, j]).wait()

    for buf, rsem, fsem in ((cbuf, cr, cfs), (vbuf, vr, vfs)):
        for dy in range(2):
            for dx in range(2):
                yy, xx = (y + dy) % 2, (x + dx) % 2
                arrived(buf, rsem, yy, 2 * xx + h)
                hand_on(buf, fsem, rsem, yy, xx).start()

    def stacked(buf, rsem, out):
        for yy in range(2):
            for xx in range(2):
                arrived(buf, rsem, yy, 2 * xx + 1 - h)
        for j in range(rows):
            for yy in range(2):
                for part in range(2):
                    block = buf[yy, j, :, part].reshape(kpd * npair, 2 * half)
                    out[j, pl.ds((2 * part + yy) * kpd * npair, kpd * npair), :] = block

    lanes = pl.ds(pl.multiple_of(h * half, half), half)
    stacked(cbuf, cr, lhs)
    for j in range(rows):
        both = lhs[j, :, lanes]
        real, imag = both[:mrows], both[mrows:]
        mix[j, :mrows, :half] = real
        mix[j, :mrows, half:] = imag
        mix[j, mrows:, :half] = -imag
        mix[j, mrows:, half:] = real

    def plain(i, j, w):
        xacc[j] += jnp.dot(mix[i], w, preferred_element_type=F32)

    def adjoint(i, j, w):
        p = nt(lhs[j], w)
        xacc[i, :mrows, lanes] += p[:mrows, :half] - p[mrows:, half:]
        xacc[i, mrows:, lanes] -= p[:mrows, half:] + p[mrows:, :half]

    def block(i, j):
        return wall[i, j].reshape(2 * half, 2 * half)

    plain(z, z, block(z, z))
    for n in range(1, rows):
        j = (z + n) % rows
        plain(z, j, block(z, j))
        adjoint(z, j, block(z, j))

    stacked(vbuf, vr, vl)

    nsq, noth = len(squares[0]), len(others[0])
    for n in range(max(nsq, noth)):
        if n < noth:
            i = pick(z, [s[n][0] for s in others])
            j = pick(z, [s[n][1] for s in others])
            for part in range(2):
                pltpu.make_async_copy(wall.at[i, j, part], wall.at[i, j, part], zr.at[i, j, part]).wait()
            plain(i, j, block(i, j))
            adjoint(i, j, block(i, j))
        if n < nsq:
            i = pick(z, [s[n][0] for s in squares])
            pltpu.make_async_copy(packed.at[i], packed.at[i], zr.at[i, i, 1]).wait()
            both = packed[i].astype(F32)
            real = jnp.where(at_col >= at_row, both, 0.0).astype(BF16)
            above = jnp.where(at_col > at_row, both, 0.0).astype(BF16)
            imag = jnp.where(at_col < at_row, both, 0.0).astype(BF16)
            plain(i, i, jnp.concatenate([real, imag], 0))
            adjoint(i, i, jnp.concatenate([above, imag], 0))

    with_real = jnp.zeros((2 * mrows, mrows), F32)
    with_imag = jnp.zeros((2 * mrows, mrows), F32)
    for j in range(rows):
        total = xacc[j]
        high = total.astype(BF16)
        low = (total - high.astype(F32)).astype(BF16)
        vreal, vimag = vl[j, :mrows], vl[j, mrows:]
        with_real += nt(high, vreal) + nt(low, vreal)
        with_imag += nt(high, vimag) + nt(low, vimag)
    kreal = with_real[:mrows] - with_imag[mrows:]
    kimag = with_imag[:mrows] + with_real[mrows:]

    width = npair * npair
    row = lax.broadcasted_iota(jnp.int32, (mrows, mrows), 0)
    col = lax.broadcasted_iota(jnp.int32, (mrows, mrows), 1)
    same_k = lax.div(row, npair) == lax.div(col, npair)
    vrow = lax.broadcasted_iota(jnp.int32, (mrows, width), 0)
    lane = lax.broadcasted_iota(jnp.int32, (mrows, width), 1)
    spread = jnp.where(lax.rem(vrow, npair) == lax.rem(lane, npair), 1.0, 0.0).astype(BF16)
    same_a = lax.rem(vrow, npair) == lax.div(lane, npair)
    kgrid = mrows // npair
    for part, value in enumerate((kreal, kimag)):
        wide = sum(
            jnp.dot(piece, spread, preferred_element_type=F32) for piece in thirds(jnp.where(same_k, value, 0.0))
        )
        wide = jnp.where(same_a, wide, 0.0).reshape(kgrid, npair, width)
        kown[pl.ds(part * kgrid, kgrid), :] = wide.sum(1)

    pair_sum = remote(kown, ksib, ks, kr, dev(z, y, x, 1 - h))
    pair_sum.start()
    pair_sum.wait()
    total = kown[...] + ksib[...]
    share = kstage.shape[2]
    for n in range(kstage.shape[0]):
        kstage[n] = total[:, n * share:(n + 1) * share]

    def out_copies():
        n = 0
        for dz in range(rows):
            for dy in range(2):
                for dx in range(2):
                    if dz or dy or dx:
                        zz, yy, xx = (z + dz) % rows, (y + dy) % 2, (x + dx) % 2
                        yield remote(
                            kstage.at[2 * xx + h], kall.at[mine, z], os.at[n], orr.at[mine, z], dev(zz, yy, xx, h)
                        )
                        n += 1

    for copy in out_copies():
        copy.start()
    kall[mine, z] = kstage[g]
    for dz in range(rows):
        for dy in range(2):
            for dx in range(2):
                if dz or dy or dx:
                    zz = (z + dz) % rows
                    qq = 2 * ((x + dx) % 2) + (y + dy) % 2
                    pltpu.make_async_copy(kall.at[qq, zz], kall.at[qq, zz], orr.at[qq, zz]).wait()

    all_ref[...] = kall[...]

    for n in range(3):
        for part in range(2):
            w_copy(n, part).wait_send()
        pair_copy(c_ref, cbuf, cs, cr, n).wait_send()
        pair_copy(v_ref, vbuf, vs, vr, n).wait_send()

    @pl.when(h != y)
    def _():
        for part in range(2):
            w_copy(3, part).wait_send()

    for src in range(rows):
        @pl.when(z == src)
        def _():
            for copy in z_copies(src):
                copy.wait_send()

    for buf, rsem, fsem in ((cbuf, cr, cfs), (vbuf, vr, vfs)):
        for dy in range(2):
            for dx in range(2):
                hand_on(buf, fsem, rsem, (y + dy) % 2, (x + dx) % 2).wait_send()
    for copy in out_copies():
        copy.wait_send()


def choose(rows, kp_ref, kall, f_ref, b_ref):
    kpd, share = f_ref.shape[1], f_ref.shape[3]
    kgrid = 2 * kpd
    ka = lax.axis_index("ka")
    z, y = ka // 2, ka % 2
    outs = 2 * kpd
    o = lax.broadcasted_iota(jnp.int32, (outs, rows * 2 * kgrid), 0)
    r = lax.broadcasted_iota(jnp.int32, (outs, rows * 2 * kgrid), 1)
    k_here = y * kpd + lax.div(o, 2)
    part_at = lax.rem(o, 2) * kgrid
    ahead = jnp.where(r == z * 2 * kgrid + part_at + k_here, 1.0, 0.0).astype(F32)
    for q in range(kall.shape[0]):
        table = kall[q].reshape(rows * 2 * kgrid, share)
        corner = kp_ref[q, 0]
        row_step = lax.div(corner, kgrid)
        col_step = lax.rem(corner, kgrid)
        src_row = lax.rem(z - row_step + rows, rows)
        src_col = lax.rem(k_here - col_step + kgrid, kgrid)
        behind = jnp.where(r == src_row * 2 * kgrid + part_at + src_col, 1.0, 0.0).astype(F32)
        choice = jnp.concatenate([ahead, behind], 0).astype(BF16)
        chosen = sum(jnp.dot(choice, piece, preferred_element_type=F32) for piece in thirds(table))
        for t in range(kpd):
            f_ref[q, t] = chosen[2 * t:2 * t + 2]
            b_ref[q, t] = chosen[outs + 2 * t:outs + 2 * t + 2]


def exchanged(cond_pairs, val_pairs, screened, k_plus):
    nq, kpd, _, npair, cols = cond_pairs.shape
    half = screened.shape[2]
    rows = lax.axis_size("ka") // 2
    ga = lax.axis_size("ga")
    mrows = 2 * kpd * npair
    width = npair * npair
    share = width // ga
    dma = pltpu.SemaphoreType.DMA
    out = jax.ShapeDtypeStruct((nq, kpd, 2, share), F32)
    squares, others = block_plan(rows)
    most = max(
        sum(i == src for d in range(rows) for i, _ in squares[d] + others[d]) for src in range(rows)
    )
    blocks = pl.pallas_call(
        functools.partial(kernel, rows),
        out_shape=jax.ShapeDtypeStruct((nq, rows, 4 * kpd, share), F32),
        in_specs=[pl.BlockSpec(memory_space=pltpu.HBM)] * 3,
        out_specs=pl.BlockSpec(memory_space=pltpu.VMEM),
        scratch_shapes=[
            pltpu.VMEM((rows, rows, 2, half, cols), BF16),
            pltpu.VMEM((rows, half, cols), BF16),
            pltpu.VMEM((2, ga, kpd, 2, npair, cols), BF16),
            pltpu.VMEM((2, ga, kpd, 2, npair, cols), BF16),
            pltpu.VMEM((ga, 2 * mrows, cols), BF16),
            pltpu.VMEM((ga, 2 * mrows, cols), BF16),
            pltpu.VMEM((ga, 2 * mrows, cols), BF16),
            pltpu.VMEM((ga, 2 * mrows, cols), F32),
            pltpu.VMEM((4 * kpd, width), F32),
            pltpu.VMEM((4 * kpd, width), F32),
            pltpu.VMEM((ga, 4 * kpd, share), F32),
            pltpu.VMEM((nq, rows, 4 * kpd, share), F32),
            dma((4, 2)), dma((ga, 2)),
            dma((3,)), dma((2, ga)),
            dma((3,)), dma((2, ga)),
            dma((2, 2)), dma((2, 2)),
            dma((most, 2)), dma((rows, rows, 2)),
            dma, dma,
            dma((4 * rows - 1,)), dma((nq, rows)),
        ],
        compiler_params=pltpu.CompilerParams(
            collective_id=0, has_side_effects=True, vmem_limit_bytes=64 * 1024 * 1024 - 320 * 1024
        ),
    )(cond_pairs, val_pairs, screened)
    return pl.pallas_call(
        functools.partial(choose, rows),
        out_shape=(out, out),
        in_specs=[pl.BlockSpec(memory_space=pltpu.SMEM), pl.BlockSpec(memory_space=pltpu.VMEM)],
        out_specs=[pl.BlockSpec(memory_space=pltpu.VMEM)] * 2,
    )(k_plus, blocks)


NG = 1024
Q = 4
npair = 16
npair = 16


def passed_along(block, axis, distance):
    devices = range(lax.axis_size(axis))
    route = [((i - distance) % len(devices), i) for i in devices]
    return lax.ppermute(block, axis, route)


def swapped(shard, axis, bit):
    return lax.ppermute(shard, axis, [(i, i ^ 1 << bit) for i in range(lax.axis_size(axis))])


def screen_fold(left_real, left_imag, piece):
    real_next = jnp.dot(left_real, piece[0], preferred_element_type=jnp.float32) + jnp.dot(
        left_imag, piece[1], preferred_element_type=jnp.float32
    )
    imag_next = jnp.dot(left_real, piece[1], preferred_element_type=jnp.float32) - jnp.dot(
        left_imag, piece[0], preferred_element_type=jnp.float32
    )
    return (real_next, imag_next)


def pair_contract(left, right):
    return jnp.einsum("kag,kbg->kab", left, right, preferred_element_type=jnp.float32)


def local(cond_pairs, val_pairs, screened, k_plus):
    nq, local_k, _, npair, own = cond_pairs.shape
    ng = own * lax.axis_size("ga")
    columns = screened.shape[3]
    grid_y = 2 * local_k
    forward = []
    for q_index in range(nq):
        cond_full = lax.all_gather(cond_pairs[q_index], "ga", axis=3, tiled=True)
        left_real = cond_full[:, 0].reshape(local_k * npair, ng)
        left_imag = cond_full[:, 1].reshape(local_k * npair, ng)
        real_x, imag_x = screen_fold(
            left_real, left_imag, lax.all_gather(screened[q_index], "ka", axis=1, tiled=True)
        )
        real_b = real_x.astype(jnp.bfloat16).reshape(local_k, npair, columns)
        imag_b = imag_x.astype(jnp.bfloat16).reshape(local_k, npair, columns)
        val_real = val_pairs[q_index][:, 0]
        val_imag = val_pairs[q_index][:, 1]
        kernel_real = pair_contract(real_b, val_real) - pair_contract(imag_b, val_imag)
        kernel_imag = pair_contract(real_b, val_imag) + pair_contract(imag_b, val_real)
        forward.append(jnp.stack([kernel_real, kernel_imag], 1).reshape(local_k, 2, npair * npair))
    partial_value = jnp.stack(forward, 0)
    total = lax.psum(partial_value, "ga")
    width = total.shape[3] // lax.axis_size("ga")
    kernel_share = lax.dynamic_slice_in_dim(total, lax.axis_index("ga") * width, width, 3)
    count = lax.axis_size("ka")
    corner = k_plus[:, 0]
    row_step = corner // grid_y
    col_step = corner % grid_y
    hop_length = 2 * row_step % count
    moved = kernel_share
    nbits = count.bit_length() - 1
    for bit_number in range(1, nbits):
        arrived = passed_along(moved, "ka", 1 << bit_number)
        taken = hop_length // (1 << bit_number) % 2 == 1
        moved = jnp.where(taken[:, None, None, None], arrived, moved)
    partner = swapped(moved, "ka", 0)
    half_index = lax.axis_index("ka") % 2
    whole_row = jnp.where(
        half_index == 0, jnp.concatenate([moved, partner], 1), jnp.concatenate([partner, moved], 1)
    )
    doubled = jnp.concatenate([whole_row, whole_row], 1)
    backs = []
    for q_index in range(nq):
        begin = (half_index * local_k - col_step[q_index] + grid_y) % grid_y
        backs.append(lax.dynamic_slice_in_dim(doubled[q_index], begin, local_k, 0))
    kernel_back = jnp.stack(backs, 0)
    return (kernel_share, kernel_back)


def solution(mesh):
    in_specs = (
        P(None, "ka", None, None, "ga"),
        P(None, "ka", None, None, "ga"),
        P(None, None, "ka", "ga"),
        P(),
    )
    out_specs = (P(None, "ka", None, "ga"), P(None, "ka", None, "ga"))
    square = mesh.shape["ga"] == 4 and mesh.shape["ka"] == 2 * mesh.shape["ga"]
    body = exchanged if square else local
    return jax.shard_map(body, mesh=mesh, in_specs=in_specs, out_specs=out_specs, check_vma=False)
```
